256 devices in a mesh: seq: 64 (over x, z, core), head: 4 (over y).
Axes of the slice: x: 4, y: 4, z: 8, core: 2. Of those that a mesh axis runs over, the one named last changes fastest.
Arguments:
- queries: bfloat16 [8192, 2048], P('seq', 'head'), may hold values from -6 to 6
- key_vecs: bfloat16 [8192, 2048], P('seq', 'head'), may hold values from -6 to 6
- values: bfloat16 [8192, 4096], P('seq', 'head'), may hold values from -6 to 6
- output_gate: bfloat16 [8192, 4096], P('seq', 'head'), may hold values from -6 to 6
- decay_gate: float32 [32, 8192], P('head', 'seq'), may hold values from 0.5 to 1
- write_rate: float32 [32, 8192], P('head', 'seq'), may hold values from 0 to 1
- initial_state: float32 [32, 128, 128], P('head'), may hold values from -0.6 to 0.6
- norm_gain: float32 [128], replicated, may hold values from 0.5 to 1.5
- out_weight: bfloat16 [4096, 2048], P('head'), may hold values from -0.09375 to 0.09375
Outputs:
- layer_out: bfloat16 [8192, 2048], P('seq', 'head')
The draws below stay inside these ranges and needn't reach their ends.
All inputs are finite; a program needn't handle non-finite values.
Results may differ from the reference program's by a relative error of at most 0.015.
Values may be sent and summed in bfloat16 or wider, within the bound.
A program may use at most 192 MiB of HBM per device.

```python
import jax
import jax.numpy as jnp
from jax import lax

D = 2048
VALUE_HEADS = 32
HK = 16
DK = 128
DV = 128
STRETCH = 128
TOK_DEV = 128
SLAB_TOKENS = 8192


def head_kinds(key, share):
    return jax.random.randint(key, (VALUE_HEADS,), 0, 10) < share


def block_factors(key):
    factors = jnp.exp(jax.random.uniform(key, (VALUE_HEADS, SLAB_TOKENS // TOK_DEV), jnp.float32, jnp.log(0.6), jnp.log(1.6)))
    return jnp.repeat(factors, TOK_DEV, axis=1)


def draw_decay_gate(key, part):
    slow = head_kinds(key, 5)
    key = jax.random.fold_in(key, 11)
    first, second, third, fourth_piece = jax.random.split(key, 4)
    factors = block_factors(first)
    base = jnp.exp(jax.random.uniform(second, (VALUE_HEADS, 1), jnp.float32, jnp.log(0.25), jnp.log(1.0)))
    slow_gate = jnp.exp(-base * factors / SLAB_TOKENS)
    span = jax.random.uniform(third, (VALUE_HEADS, 1), jnp.float32, 30.0, 50.0)
    fast_gate = jnp.exp(-factors / span)
    gate_factor = jnp.where(slow[:, None], slow_gate, fast_gate)
    token_group = jax.random.randint(fourth_piece, (VALUE_HEADS, SLAB_TOKENS), 0, SLAB_TOKENS) < 2
    group_values = jax.random.uniform(jax.random.fold_in(key, 5), (VALUE_HEADS, SLAB_TOKENS), jnp.float32, 0.5, 0.8)
    return jnp.where(token_group, group_values, gate_factor)


def draw_write_rate(key, part):
    slow = head_kinds(key, 5)
    fast_low = 0.3
    key = jax.random.fold_in(key, 12)
    first, second = jax.random.split(key, 2)
    slow_rate = DK / SLAB_TOKENS * jnp.exp(jax.random.uniform(first, (VALUE_HEADS, SLAB_TOKENS), jnp.float32, jnp.log(0.25), jnp.log(1.0)))
    fast_rate = jax.random.uniform(second, (VALUE_HEADS, SLAB_TOKENS), jnp.float32, fast_low, 1.0)
    return jnp.where(slow[:, None], slow_rate, fast_rate)


def levels(key, shape, cuts, low, largest):
    def one(axis_at, blocks):
        draws = jax.random.uniform(jax.random.fold_in(jax.random.fold_in(key, 6), axis_at), (blocks,), jnp.float32, low / len(cuts), largest / len(cuts))
        return jnp.repeat(jnp.exp(draws), shape[axis_at] // blocks).reshape((-1,) + (1,) * (len(shape) - axis_at - 1))

    level = one(*cuts[0])
    for cut in cuts[1:]:
        level = level * one(*cut)
    return level


def bell_draw(rng, extent, spread, most, cuts=(), kind=jnp.bfloat16):
    drawn = jax.random.normal(rng, extent, jnp.float32) * spread
    if len(cuts) > 0:
        drawn = levels(rng, extent, cuts, -0.22, 0.18) * drawn
    return jnp.clip(drawn, min=-most, max=most).astype(kind)


def setup_inputs(seed: int = 0) -> dict:
    key_list = jax.random.split(jax.random.key(seed), 10)
    queries = bell_draw(key_list[0], (SLAB_TOKENS, HK * DK), 1.0, 6.0, ((0, 64), (1, 4)))
    key_vecs = bell_draw(key_list[1], (SLAB_TOKENS, HK * DK), 1.0, 6.0, ((0, 64), (1, 4)))
    values = bell_draw(key_list[2], (SLAB_TOKENS, VALUE_HEADS * DV), 1.0, 6.0, ((0, 64), (1, 4)))
    output_gate = bell_draw(key_list[3], (SLAB_TOKENS, VALUE_HEADS * DV), 1.0, 6.0, ((0, 64), (1, 4)))
    decay_gate = draw_decay_gate(jax.random.fold_in(key_list[9], 71), 0)
    write_rate = draw_write_rate(jax.random.fold_in(key_list[9], 71), 0)
    initial_state = bell_draw(key_list[6], (VALUE_HEADS, DK, DV), 0.1, 0.6, ((0, 4),), jnp.float32)
    norm_gain = jnp.clip(1.0 + 0.1 * jax.random.normal(key_list[7], (DV,), jnp.float32), 0.5, 1.5)
    out_weight = bell_draw(key_list[8], (VALUE_HEADS * DV, D), (VALUE_HEADS * DV) ** -0.5, 0.09375, ((0, 4),))
    return {"queries": queries, "key_vecs": key_vecs, "values": values, "output_gate": output_gate, "decay_gate": decay_gate, "write_rate": write_rate, "initial_state": initial_state, "norm_gain": norm_gain, "out_weight": out_weight}


HIGH = lax.Precision.HIGHEST

def unit_heads(block, heads):
    rows = block.astype(jnp.float32).reshape(block.shape[0], heads, -1).transpose(1, 0, 2)
    return rows / jnp.sqrt(lax.optimization_barrier(jnp.sum(rows * rows, axis=-1, keepdims=True)) + 1e-06)

def stretch_terms(query_unit, key_unit, vals, logs, rates):
    size = logs.shape[-1]
    width = key_unit.shape[-1]
    row_ids = lax.broadcasted_iota(jnp.int32, (size, size), 0)
    column_index = lax.broadcasted_iota(jnp.int32, (size, size), 1)
    strict = row_ids > column_index
    within = row_ids >= column_index
    lower_ones = within.astype(logs.dtype)
    cum = jnp.einsum('...j,ij->...i', logs, lower_ones, precision=HIGH)
    diff = cum[..., :, None] - cum[..., None, :]
    weighted = key_unit * rates[..., None]
    inner = jnp.einsum('...id,...jd->...ij', weighted, key_unit, precision=HIGH)
    lower_part = jnp.where(strict, inner * jnp.exp(jnp.where(strict, diff, 0.0)), 0.0)
    system = lower_part + jnp.eye(size, dtype=logs.dtype)
    right = jnp.concatenate([weighted * jnp.exp(cum)[..., None], vals * rates[..., None]], axis=-1)
    solved = jax.scipy.linalg.solve_triangular(system, right, lower=True, unit_diagonal=True)
    w_part = solved[..., :width]
    u_part = solved[..., width:]
    scaled_q = query_unit * width ** (-0.5)
    scores = jnp.einsum('...id,...jd->...ij', scaled_q, key_unit, precision=HIGH)
    scores = jnp.where(within, scores * jnp.exp(jnp.where(within, diff, 0.0)), 0.0)
    readout = scaled_q * jnp.exp(cum)[..., None] - jnp.einsum('...ij,...jd->...id', scores, w_part, precision=HIGH)
    local_out = jnp.einsum('...ij,...je->...ie', scores, u_part, precision=HIGH)
    last = cum[..., -1]
    carried = key_unit * jnp.exp(last[..., None] - cum)[..., None]
    trans = jnp.exp(last)[..., None, None] * jnp.eye(width, dtype=logs.dtype) - jnp.einsum('...id,...ie->...de', carried, w_part, precision=HIGH)
    bias = jnp.einsum('...id,...ie->...de', carried, u_part, precision=HIGH)
    return (readout, local_out, trans, bias)

def gated_norm(out, gate_rows, norm_gain):
    heads = out.shape[0]
    mixed = out.transpose(1, 0, 2)
    scaled = mixed / jnp.sqrt(lax.optimization_barrier(jnp.mean(mixed * mixed, axis=-1, keepdims=True)) + 1e-06) * norm_gain
    gate_vals = gate_rows.astype(jnp.float32).reshape(gate_rows.shape[0], heads, -1)
    return (scaled * jax.nn.silu(gate_vals)).reshape(gate_rows.shape[0], -1).astype(jnp.bfloat16)

def reference(queries, key_vecs, values, output_gate, decay_gate, write_rate, initial_state, norm_gain, out_weight):
    count = SLAB_TOKENS // STRETCH
    group = VALUE_HEADS // HK
    blocks = (queries.reshape(count, STRETCH, -1), key_vecs.reshape(count, STRETCH, -1), values.reshape(count, STRETCH, -1), output_gate.reshape(count, STRETCH, -1), decay_gate.reshape(VALUE_HEADS, count, STRETCH).transpose(1, 0, 2), write_rate.reshape(VALUE_HEADS, count, STRETCH).transpose(1, 0, 2))

    def advance(state, block):
        q_rows, k_rows, v_rows, g_rows, decay_rows, rate_rows = block
        query_unit = jnp.repeat(unit_heads(q_rows, HK), group, axis=0)
        key_unit = jnp.repeat(unit_heads(k_rows, HK), group, axis=0)
        vals = v_rows.astype(jnp.float32).reshape(STRETCH, VALUE_HEADS, DV).transpose(1, 0, 2)
        readout, local_out, trans, bias = stretch_terms(query_unit, key_unit, vals, jnp.log(decay_rows), rate_rows)
        out = jnp.einsum('hcd,hde->hce', readout, state, precision=HIGH) + local_out
        fresh = jnp.einsum('hde,hef->hdf', trans, state, precision=HIGH) + bias
        return (fresh, gated_norm(out, g_rows, norm_gain))
    _, normalized_rows = lax.scan(advance, initial_state, blocks)
    normalized_rows = normalized_rows.reshape(SLAB_TOKENS, VALUE_HEADS * DV)
    return jnp.dot(normalized_rows.astype(jnp.float32), out_weight.astype(jnp.float32), preferred_element_type=jnp.float32).astype(jnp.bfloat16)
```

```python
import functools

import jax
import jax.numpy as jnp
from jax import lax
from jax.experimental import pallas as pl
from jax.experimental.pallas import tpu as pltpu
from jax.sharding import PartitionSpec as P

MESH = pl.DeviceIdType.MESH
F32 = jnp.float32
BF16 = jnp.bfloat16
HEADS = 8
KEYS = 4
C = 128
NX = 4
NZ = 8
NY = 4
HALF = HEADS // 2
MSG = 2 * C + 16
OUT = 512


def mm(a, b):
    return lax.dot_general(a, b, (((1,), (0,)), ((), ())), preferred_element_type=F32)


def mm_t(a, b):
    return lax.dot_general(a, b, (((1,), (1,)), ((), ())), preferred_element_type=F32)


def put_gain(ref, index, gain):
    wide = jnp.broadcast_to(gain, (8, C))
    high = wide.astype(BF16).astype(F32)
    ref[index, 2 * C :, :] = jnp.concatenate([high, wide - high], axis=0).astype(BF16)


def get_gain(ref, index):
    rows = ref[index, 2 * C :, :].astype(F32)
    return rows[0:1, :] + rows[8:9, :]


def kernel(
    q_ref,
    k_ref,
    v_ref,
    gate_hbm,
    decay_ref,
    rate_ref,
    init_hbm,
    gain_ref,
    weight_hbm,
    out_ref,
    gate_ref,
    init_ref,
    weight_ref,
    wu_ref,
    score_ref,
    read_ref,
    local_ref,
    silu_ref,
    own,
    sib,
    comb,
    chain,
    total,
    prefix_d,
    prefix_c,
    prefix_g,
    state,
    give,
    take,
    normed,
    part,
    parts,
    load_sem,
    sib_send,
    sib_recv,
    comb_send,
    chain_recv,
    total_send,
    total_recv,
    give_send,
    take_recv,
    part_send,
    parts_recv,
):
    seq, y = lax.axis_index("seq"), lax.axis_index("head")
    x, z, c = seq // 16, lax.rem(seq // 2, NZ), lax.rem(seq, 2)
    base = x * 16
    other = base + z * 2 + (1 - c)

    def remote(src, dst, send, recv, to_seq, to_y):
        return pltpu.make_async_remote_copy(
            src_ref=src,
            dst_ref=dst,
            send_sem=send,
            recv_sem=recv,
            device_id=(to_seq, to_y),
            device_id_type=MESH,
        )

    barrier = pltpu.get_barrier_semaphore()
    for step in range(1, 16):
        pl.semaphore_signal(
            barrier, inc=1, device_id=(base + lax.rem(z * 2 + c + step, 16), y), device_id_type=MESH
        )
    for step in range(1, NX):
        pl.semaphore_signal(
            barrier, inc=1, device_id=(lax.rem(seq + 16 * step, 64), y), device_id_type=MESH
        )
    for step in range(1, NY):
        pl.semaphore_signal(
            barrier, inc=1, device_id=(seq, lax.rem(y + step, NY)), device_id_type=MESH
        )
    loads = [
        pltpu.make_async_copy(init_hbm, init_ref, load_sem.at[0]),
        pltpu.make_async_copy(gate_hbm, gate_ref, load_sem.at[1]),
        pltpu.make_async_copy(weight_hbm, weight_ref, load_sem.at[2]),
    ]
    for load in loads:
        load.start()

    rows = lax.broadcasted_iota(jnp.int32, (C, C), 0)
    cols = lax.broadcasted_iota(jnp.int32, (C, C), 1)
    apart = rows ^ cols
    strict = rows > cols
    within = rows >= cols
    diagonal = (rows == cols).astype(F32)
    upto = (rows <= cols).astype(BF16)
    logs = jnp.log(decay_ref[...])
    rates = rate_ref[...]
    high = logs.astype(BF16)
    rest = logs - high.astype(F32)
    middle = rest.astype(BF16)
    low = (rest - middle.astype(F32)).astype(BF16)
    cum = mm(high, upto) + (mm(middle, upto) + mm(low, upto))
    tall = jnp.concatenate([cum, rates, jnp.zeros((C - 2 * HEADS, C), F32)], axis=0).T
    ends = [cum[h : h + 1, C - 1 : C] for h in range(HEADS)]

    lower, inverse, row_keys, col_keys = [], [], [], []
    for kh in range(KEYS):
        keys = k_ref[:, kh * C : (kh + 1) * C]
        asks = q_ref[:, kh * C : (kh + 1) * C]
        inner = mm_t(keys, keys)
        cross = mm_t(asks, keys)
        squares = inner * diagonal
        row_key = lax.rsqrt(jnp.sum(squares, axis=0, keepdims=True) + 1e-6)
        col_key = lax.rsqrt(jnp.sum(squares, axis=1, keepdims=True) + 1e-6)
        wide_asks = asks.astype(F32)
        col_ask = lax.rsqrt(jnp.sum(wide_asks * wide_asks, axis=1, keepdims=True) + 1e-6)
        col_ask = col_ask * (C**-0.5)
        row_keys.append(row_key)
        col_keys.append(col_key)
        for h in (2 * kh, 2 * kh + 1):
            cum_col = tall[:, h : h + 1]
            rate_col = tall[:, HEADS + h : HEADS + h + 1]
            fade = jnp.exp(jnp.where(within, cum_col - cum[h : h + 1, :], 0.0))
            fade = fade * row_key
            low_part = jnp.where(strict, inner * fade * (rate_col * col_key), 0.0).astype(BF16)
            lower.append(low_part)
            score_ref[h] = jnp.where(within, cross * fade * col_ask, 0.0).astype(BF16)
            read_ref[h] = wide_asks * (col_ask * jnp.exp(cum_col))
            inverse.append(jnp.where(apart == 1, -low_part.astype(F32), diagonal).astype(BF16))
    size = 2
    while size < C:
        mask = ((apart >= size) & (apart < 2 * size)).astype(BF16)
        firsts = [mm(inverse[h], lower[h] * mask).astype(BF16) for h in range(HEADS)]
        inverse = [inverse[h] - mm(firsts[h], inverse[h]).astype(BF16) for h in range(HEADS)]
        size *= 2
    for kh in range(KEYS):
        keys = k_ref[:, kh * C : (kh + 1) * C]
        keys_t = keys.astype(F32).T.astype(BF16)
        for h in (2 * kh, 2 * kh + 1):
            wide = inverse[h].astype(F32)
            rate_row = rates[h : h + 1, :]
            cum_row = cum[h : h + 1, :]
            w_part = mm((wide * (rate_row * jnp.exp(cum_row) * row_keys[kh])).astype(BF16), keys)
            u_part = mm((wide * rate_row).astype(BF16), v_ref[:, h * C : (h + 1) * C])
            both = jnp.concatenate([w_part, u_part], axis=1)
            wu_ref[h] = both.astype(BF16)
            fade_col = col_keys[kh] * jnp.exp(ends[h] - tall[:, h : h + 1])
            maps = mm(keys_t, (both * fade_col).astype(BF16))
            own[h, 0:C, :] = maps[:, 0:C].astype(BF16)
            own[h, C : 2 * C, :] = maps[:, C:].astype(BF16)
            put_gain(own, h, jnp.exp(ends[h]))

    pl.semaphore_wait(barrier, 15 + NX - 1 + NY - 1)

    to_other = [
        remote(own.at[h], sib.at[h], sib_send.at[h], sib_recv.at[h], other, y)
        for h in range(HEADS)
    ]

    @pl.when(c == 0)
    def _():
        for h in range(HALF, HEADS):
            to_other[h].start()

    for h in range(HALF):
        to_other[h].start()

    def joined(index):
        h = c * HALF + index
        remote(own.at[h], sib.at[h], sib_send.at[h], sib_recv.at[h], other, y).wait_recv()
        mine, theirs = own[h, 0 : 2 * C, :], sib[h, 0 : 2 * C, :]
        my_gain, their_gain = get_gain(own, h), get_gain(sib, h)
        first = c == 0
        early = jnp.where(first, mine.astype(F32), theirs.astype(F32))
        late = jnp.where(first, theirs.astype(F32), mine.astype(F32))
        early_gain = jnp.where(first, my_gain, their_gain)
        late_gain = jnp.where(first, their_gain, my_gain)
        late_map = late[0:C].astype(BF16)
        pair = jnp.concatenate([early[0:C], early[C:]], axis=1).astype(BF16)
        moved = mm(late_map, pair)
        comb[index, 0:C, :] = (
            late_gain * early[0:C] + early_gain * late[0:C] - moved[:, 0:C]
        ).astype(BF16)
        comb[index, C : 2 * C, :] = (late_gain * early[C:] + late[C:] - moved[:, C:]).astype(BF16)
        put_gain(comb, index, early_gain * late_gain)

    def to_chain(index):
        h = c * HALF + index
        return remote(
            comb.at[index],
            chain.at[z],
            comb_send.at[index],
            chain_recv.at[z],
            base + h * 2 + c,
            y,
        )

    for index in range(HALF):
        joined(index)

        @pl.when(z != c * HALF + index)
        def _():
            to_chain(index).start()

        @pl.when(z == c * HALF + index)
        def _():
            chain[z] = comb[index]

    for h in range(HEADS):
        pair = mm(score_ref[h], wu_ref[h])
        read_ref[h] = read_ref[h] - pair[:, 0:C]
        local_ref[h] = pair[:, C:]
    loads[1].wait()
    gate = gate_ref[...].astype(F32)
    gains = jnp.concatenate([gain_ref[...]] * HEADS, axis=1)
    silu_ref[...] = gate / (1.0 + jnp.exp(-gate)) * gains
    loads[0].wait()
    loads[2].wait()

    works = z // HALF == c

    def to_segment(step):
        return remote(
            total.at[x],
            total.at[x],
            total_send.at[step],
            total_recv.at[x],
            lax.rem(seq + 16 * step, 64),
            y,
        )

    def to_chip(j, core):
        return remote(
            give.at[j],
            take.at[z],
            give_send.at[j * 2 + core],
            take_recv.at[z],
            base + j * 2 + core,
            y,
        )

    @pl.when(works)
    def _():
        d_now = jnp.zeros((C, C), F32)
        c_now = jnp.zeros((C, C), F32)
        g_now = jnp.ones((1, C), F32)
        for j in range(NZ):

            @pl.when(z != j)
            def _():
                remote(
                    chain.at[j], chain.at[j], comb_send.at[0], chain_recv.at[j], other, y
                ).wait_recv()

            prefix_d[j] = d_now.astype(BF16)
            prefix_c[j] = c_now
            prefix_g[j] = jnp.broadcast_to(g_now, (8, C))
            step_map = chain[j, 0:C, :]
            step_bias = chain[j, C : 2 * C, :].astype(F32)
            gain = get_gain(chain, j)
            wide_map = step_map.astype(F32)
            if j == 0:
                d_now, c_now = wide_map, step_bias
            else:
                moved = mm(step_map, jnp.concatenate([d_now, c_now], axis=1).astype(BF16))
                d_now = gain * d_now + g_now * wide_map - moved[:, 0:C]
                c_now = gain * c_now + step_bias - moved[:, C:]
            g_now = g_now * gain
        total[x, 0:C, :] = d_now.astype(BF16)
        total[x, C : 2 * C, :] = c_now.astype(BF16)
        put_gain(total, x, g_now)
        for step in range(1, NX):

            @pl.when(x + step < NX)
            def _():
                to_segment(step).start()

        state[...] = init_ref[z]
        for before in range(NX - 1):

            @pl.when(before < x)
            def _():
                remote(
                    total.at[before],
                    total.at[before],
                    total_send.at[0],
                    total_recv.at[before],
                    other,
                    y,
                ).wait_recv()
                now = state[...]
                state[...] = (
                    get_gain(total, before) * now
                    - mm(total[before, 0:C, :], now.astype(BF16))
                    + total[before, C : 2 * C, :].astype(F32)
                )

        entry = state[...]
        narrow = entry.astype(BF16)
        for j in range(NZ):
            here = prefix_g[j][0:1, :] * entry - mm(prefix_d[j], narrow) + prefix_c[j]
            give[j] = here.astype(BF16)
            for core in range(2):

                @pl.when((z != j) | (c != core))
                def _():
                    to_chip(j, core).start()

        take[z] = give[z]

    @pl.when(c == 1)
    def _():
        for h in range(HALF):
            to_other[h].wait_recv()

    for h in range(HEADS):

        @pl.when(jnp.logical_not(works) | (z != h))
        def _():
            remote(take.at[h], take.at[h], give_send.at[0], take_recv.at[h], other, y).wait_recv()

        @pl.when(c == 1)
        def _():
            now = take[h]
            here = (
                get_gain(sib, h) * now.astype(F32)
                - mm(sib[h, 0:C, :], now)
                + sib[h, C : 2 * C, :].astype(F32)
            )
            take[h] = here.astype(BF16)

        o = mm(read_ref[h].astype(BF16), take[h]) + local_ref[h]
        scale = lax.rsqrt(jnp.sum(o * o, axis=1, keepdims=True) * (1.0 / C) + 1e-6)
        normed[:, h * C : (h + 1) * C] = (o * scale * silu_ref[:, h * C : (h + 1) * C]).astype(BF16)

    def columns(to_y):
        return weight_ref[:, pl.ds(pl.multiple_of(to_y * OUT, OUT), OUT)]

    def to_row(step):
        return remote(
            part.at[step],
            parts.at[step],
            part_send.at[step],
            parts_recv.at[step],
            seq,
            lax.rem(y + step, NY),
        )

    for step in (2, 1, 3):
        part[step] = mm(normed[...], columns(lax.rem(y + step, NY))).astype(BF16)
        to_row(step).start()
    mine = mm(normed[...], columns(y))
    for step in (1, 3, 2):
        to_row(step).wait_recv()
        mine = mine + parts[step].astype(F32)
    out_ref[...] = mine.astype(BF16)

    for step in (2, 1, 3):
        to_row(step).wait_send()
    for h in range(HALF):
        to_other[h].wait_send()

    @pl.when(c == 0)
    def _():
        for h in range(HALF, HEADS):
            to_other[h].wait_send()

    for index in range(HALF):

        @pl.when(z != c * HALF + index)
        def _():
            to_chain(index).wait_send()

    @pl.when(works)
    def _():
        for step in range(1, NX):

            @pl.when(x + step < NX)
            def _():
                to_segment(step).wait_send()

        for j in range(NZ):
            for core in range(2):

                @pl.when((z != j) | (c != core))
                def _():
                    to_chip(j, core).wait_send()


def on_device(q, k, v, gate, decay, rate, init, gain, weight):
    vmem = pl.BlockSpec(memory_space=pltpu.VMEM)
    anywhere = pl.BlockSpec(memory_space=pl.ANY)
    dma = pltpu.SemaphoreType.DMA
    return pl.pallas_call(
        kernel,
        out_shape=jax.ShapeDtypeStruct((C, OUT), BF16),
        in_specs=[vmem, vmem, vmem, anywhere, vmem, vmem, anywhere, vmem, anywhere],
        out_specs=vmem,
        scratch_shapes=[
            pltpu.VMEM((C, HEADS * C), BF16),
            pltpu.VMEM((HEADS, C, C), F32),
            pltpu.VMEM((HEADS * C, NY * OUT), BF16),
            pltpu.VMEM((HEADS, C, 2 * C), BF16),
            pltpu.VMEM((HEADS, C, C), BF16),
            pltpu.VMEM((HEADS, C, C), F32),
            pltpu.VMEM((HEADS, C, C), F32),
            pltpu.VMEM((C, HEADS * C), F32),
            pltpu.VMEM((HEADS, MSG, C), BF16),
            pltpu.VMEM((HEADS, MSG, C), BF16),
            pltpu.VMEM((HALF, MSG, C), BF16),
            pltpu.VMEM((NZ, MSG, C), BF16),
            pltpu.VMEM((NX, MSG, C), BF16),
            pltpu.VMEM((NZ, C, C), BF16),
            pltpu.VMEM((NZ, C, C), F32),
            pltpu.VMEM((NZ, 8, C), F32),
            pltpu.VMEM((C, C), F32),
            pltpu.VMEM((NZ, C, C), BF16),
            pltpu.VMEM((HEADS, C, C), BF16),
            pltpu.VMEM((C, HEADS * C), BF16),
            pltpu.VMEM((NY, C, OUT), BF16),
            pltpu.VMEM((NY, C, OUT), BF16),
            dma((3,)),
            dma((HEADS,)),
            dma((HEADS,)),
            dma((HALF,)),
            dma((NZ,)),
            dma((NX,)),
            dma((NX,)),
            dma((2 * NZ,)),
            dma((HEADS,)),
            dma((NY,)),
            dma((NY,)),
        ],
        compiler_params=pltpu.CompilerParams(
            collective_id=0, has_side_effects=True, vmem_limit_bytes=40 * 2**20
        ),
        cost_estimate=pl.CostEstimate(
            flops=2 * 10**9, bytes_accessed=6 * 10**6, transcendentals=10**6
        ),
    )(q, k, v, gate, decay, rate, init, gain.reshape(1, C), weight)


def solution(mesh):
    return jax.shard_map(
        on_device,
        mesh=mesh,
        in_specs=(
            P("seq", "head"),
            P("seq", "head"),
            P("seq", "head"),
            P("seq", "head"),
            P("head", "seq"),
            P("head", "seq"),
            P("head", None, None),
            P(),
            P("head", None),
        ),
        out_specs=P("seq", "head"),
        check_vma=False,
    )
```

```python
import functools

import jax
import jax.numpy as jnp
from jax import lax
from jax.experimental import pallas as pl
from jax.experimental.pallas import tpu as pltpu
from jax.sharding import PartitionSpec as P

MESH = pl.DeviceIdType.MESH
F32 = jnp.float32
BF16 = jnp.bfloat16
HEADS = 8
KEYS = 4
C = 128
NX = 4
NZ = 8
NY = 4
HALF = HEADS // 2
MSG = 2 * C + 16
OUT = 512


def mm(a, b):
    return lax.dot_general(a, b, (((1,), (0,)), ((), ())), preferred_element_type=F32)


def mm_t(a, b):
    return lax.dot_general(a, b, (((1,), (1,)), ((), ())), preferred_element_type=F32)


def put_gain(ref, index, gain):
    wide = jnp.broadcast_to(gain, (8, C))
    high = wide.astype(BF16).astype(F32)
    ref[index, 2 * C :, :] = jnp.concatenate([high, wide - high], axis=0).astype(BF16)


def get_gain(ref, index):
    rows = ref[index, 2 * C :, :].astype(F32)
    return rows[0:1, :] + rows[8:9, :]


def kernel(
    q_hbm,
    k_hbm,
    v_hbm,
    gate_hbm,
    decay_hbm,
    rate_hbm,
    init_hbm,
    gain_hbm,
    weight_hbm,
    out_ref,
    q_ref,
    k_ref,
    v_ref,
    gate_ref,
    decay_ref,
    rate_ref,
    init_ref,
    gain_ref,
    weight_ref,
    wu_ref,
    score_ref,
    read_ref,
    local_ref,
    silu_ref,
    own,
    sib,
    comb,
    chain,
    total,
    prefix_d,
    prefix_c,
    prefix_g,
    state,
    give,
    take,
    normed,
    part,
    parts,
    load_sem,
    sib_send,
    sib_recv,
    comb_send,
    chain_recv,
    total_send,
    total_recv,
    give_send,
    take_recv,
    part_send,
    parts_recv,
):
    seq, y = lax.axis_index("seq"), lax.axis_index("head")
    x, z, c = seq // 16, lax.rem(seq // 2, NZ), lax.rem(seq, 2)
    base = x * 16
    other = base + z * 2 + (1 - c)

    def remote(src, dst, send, recv, to_seq, to_y):
        return pltpu.make_async_remote_copy(
            src_ref=src,
            dst_ref=dst,
            send_sem=send,
            recv_sem=recv,
            device_id=(to_seq, to_y),
            device_id_type=MESH,
        )

    pairs = (
        (decay_hbm, decay_ref),
        (rate_hbm, rate_ref),
        (k_hbm, k_ref),
        (q_hbm, q_ref),
        (v_hbm, v_ref),
        (gate_hbm, gate_ref),
        (gain_hbm, gain_ref),
        (init_hbm, init_ref),
        (weight_hbm, weight_ref),
    )
    loads = [
        pltpu.make_async_copy(src, dst, load_sem.at[i]) for i, (src, dst) in enumerate(pairs)
    ]
    for load in loads:
        load.start()
    barrier = pltpu.get_barrier_semaphore()
    for step in range(1, 16):
        pl.semaphore_signal(
            barrier, inc=1, device_id=(base + lax.rem(z * 2 + c + step, 16), y), device_id_type=MESH
        )
    for step in range(1, NX):
        pl.semaphore_signal(
            barrier, inc=1, device_id=(lax.rem(seq + 16 * step, 64), y), device_id_type=MESH
        )
    for step in range(1, NY):
        pl.semaphore_signal(
            barrier, inc=1, device_id=(seq, lax.rem(y + step, NY)), device_id_type=MESH
        )

    rows = lax.broadcasted_iota(jnp.int32, (C, C), 0)
    cols = lax.broadcasted_iota(jnp.int32, (C, C), 1)
    apart = rows ^ cols
    strict = rows > cols
    within = rows >= cols
    diagonal = (rows == cols).astype(F32)
    upto = (rows <= cols).astype(BF16)
    for load in loads[0:5]:
        load.wait()
    logs = jnp.log(decay_ref[...])
    rates = rate_ref[...]
    high = logs.astype(BF16)
    rest = logs - high.astype(F32)
    middle = rest.astype(BF16)
    low = (rest - middle.astype(F32)).astype(BF16)
    cum = mm(high, upto) + (mm(middle, upto) + mm(low, upto))
    tall = jnp.concatenate([cum, rates, jnp.zeros((C - 2 * HEADS, C), F32)], axis=0).T
    ends = [cum[h : h + 1, C - 1 : C] for h in range(HEADS)]

    lower, inverse, row_keys, col_keys = [], [], [], []
    for kh in range(KEYS):
        keys = k_ref[:, kh * C : (kh + 1) * C]
        asks = q_ref[:, kh * C : (kh + 1) * C]
        inner = mm_t(keys, keys)
        cross = mm_t(asks, keys)
        squares = inner * diagonal
        row_key = lax.rsqrt(jnp.sum(squares, axis=0, keepdims=True) + 1e-6)
        col_key = lax.rsqrt(jnp.sum(squares, axis=1, keepdims=True) + 1e-6)
        wide_asks = asks.astype(F32)
        col_ask = lax.rsqrt(jnp.sum(wide_asks * wide_asks, axis=1, keepdims=True) + 1e-6)
        col_ask = col_ask * (C**-0.5)
        row_keys.append(row_key)
        col_keys.append(col_key)
        for h in (2 * kh, 2 * kh + 1):
            cum_col = tall[:, h : h + 1]
            rate_col = tall[:, HEADS + h : HEADS + h + 1]
            fade = jnp.exp(jnp.where(within, cum_col - cum[h : h + 1, :], 0.0))
            fade = fade * row_key
            low_part = jnp.where(strict, inner * fade * (rate_col * col_key), 0.0).astype(BF16)
            lower.append(low_part)
            score_ref[h] = jnp.where(within, cross * fade * col_ask, 0.0).astype(BF16)
            read_ref[h] = wide_asks * (col_ask * jnp.exp(cum_col))
            inverse.append(jnp.where(apart == 1, -low_part.astype(F32), diagonal).astype(BF16))
    size = 2
    while size < C:
        mask = ((apart >= size) & (apart < 2 * size)).astype(BF16)
        firsts = [mm(inverse[h], lower[h] * mask).astype(BF16) for h in range(HEADS)]
        inverse = [inverse[h] - mm(firsts[h], inverse[h]).astype(BF16) for h in range(HEADS)]
        size *= 2
    for kh in range(KEYS):
        keys = k_ref[:, kh * C : (kh + 1) * C]
        keys_t = keys.astype(F32).T.astype(BF16)
        for h in (2 * kh, 2 * kh + 1):
            wide = inverse[h].astype(F32)
            rate_row = rates[h : h + 1, :]
            cum_row = cum[h : h + 1, :]
            w_part = mm((wide * (rate_row * jnp.exp(cum_row) * row_keys[kh])).astype(BF16), keys)
            u_part = mm((wide * rate_row).astype(BF16), v_ref[:, h * C : (h + 1) * C])
            both = jnp.concatenate([w_part, u_part], axis=1)
            wu_ref[h] = both.astype(BF16)
            fade_col = col_keys[kh] * jnp.exp(ends[h] - tall[:, h : h + 1])
            maps = mm(keys_t, (both * fade_col).astype(BF16))
            own[h, 0:C, :] = maps[:, 0:C].astype(BF16)
            own[h, C : 2 * C, :] = maps[:, C:].astype(BF16)
            put_gain(own, h, jnp.exp(ends[h]))

    pl.semaphore_wait(barrier, 15 + NX - 1 + NY - 1)

    to_other = [
        remote(own.at[h], sib.at[h], sib_send.at[h], sib_recv.at[h], other, y)
        for h in range(HEADS)
    ]

    @pl.when(c == 0)
    def _():
        for h in range(HALF, HEADS):
            to_other[h].start()

    for h in range(HALF):
        to_other[h].start()

    def joined(index):
        h = c * HALF + index
        remote(own.at[h], sib.at[h], sib_send.at[h], sib_recv.at[h], other, y).wait_recv()
        mine, theirs = own[h, 0 : 2 * C, :], sib[h, 0 : 2 * C, :]
        my_gain, their_gain = get_gain(own, h), get_gain(sib, h)
        first = c == 0
        early = jnp.where(first, mine.astype(F32), theirs.astype(F32))
        late = jnp.where(first, theirs.astype(F32), mine.astype(F32))
        early_gain = jnp.where(first, my_gain, their_gain)
        late_gain = jnp.where(first, their_gain, my_gain)
        late_map = late[0:C].astype(BF16)
        pair = jnp.concatenate([early[0:C], early[C:]], axis=1).astype(BF16)
        moved = mm(late_map, pair)
        comb[index, 0:C, :] = (
            late_gain * early[0:C] + early_gain * late[0:C] - moved[:, 0:C]
        ).astype(BF16)
        comb[index, C : 2 * C, :] = (late_gain * early[C:] + late[C:] - moved[:, C:]).astype(BF16)
        put_gain(comb, index, early_gain * late_gain)

    def to_chain(index):
        h = c * HALF + index
        return remote(
            comb.at[index],
            chain.at[z],
            comb_send.at[index],
            chain_recv.at[z],
            base + h * 2 + c,
            y,
        )

    for index in range(HALF):
        joined(index)

        @pl.when(z != c * HALF + index)
        def _():
            to_chain(index).start()

        @pl.when(z == c * HALF + index)
        def _():
            chain[z] = comb[index]

    for h in range(HEADS):
        pair = mm(score_ref[h], wu_ref[h])
        read_ref[h] = read_ref[h] - pair[:, 0:C]
        local_ref[h] = pair[:, C:]
    for load in loads[5:]:
        load.wait()
    gate = gate_ref[...].astype(F32)
    gains = jnp.concatenate([gain_ref[...]] * HEADS, axis=1)
    silu_ref[...] = gate / (1.0 + jnp.exp(-gate)) * gains

    works = z // HALF == c

    def to_segment(step):
        return remote(
            total.at[x],
            total.at[x],
            total_send.at[step],
            total_recv.at[x],
            lax.rem(seq + 16 * step, 64),
            y,
        )

    def to_chip(j, core):
        return remote(
            give.at[j],
            take.at[z],
            give_send.at[j * 2 + core],
            take_recv.at[z],
            base + j * 2 + core,
            y,
        )

    @pl.when(works)
    def _():
        d_now = jnp.zeros((C, C), F32)
        c_now = jnp.zeros((C, C), F32)
        g_now = jnp.ones((1, C), F32)
        for j in range(NZ):

            @pl.when(z != j)
            def _():
                remote(
                    chain.at[j], chain.at[j], comb_send.at[0], chain_recv.at[j], other, y
                ).wait_recv()

            prefix_d[j] = d_now.astype(BF16)
            prefix_c[j] = c_now
            prefix_g[j] = jnp.broadcast_to(g_now, (8, C))
            step_map = chain[j, 0:C, :]
            step_bias = chain[j, C : 2 * C, :].astype(F32)
            gain = get_gain(chain, j)
            wide_map = step_map.astype(F32)
            if j == 0:
                d_now, c_now = wide_map, step_bias
            else:
                moved = mm(step_map, jnp.concatenate([d_now, c_now], axis=1).astype(BF16))
                d_now = gain * d_now + g_now * wide_map - moved[:, 0:C]
                c_now = gain * c_now + step_bias - moved[:, C:]
            g_now = g_now * gain
        total[x, 0:C, :] = d_now.astype(BF16)
        total[x, C : 2 * C, :] = c_now.astype(BF16)
        put_gain(total, x, g_now)
        for step in range(1, NX):

            @pl.when(x + step < NX)
            def _():
                to_segment(step).start()

        state[...] = init_ref[z]
        for before in range(NX - 1):

            @pl.when(before < x)
            def _():
                remote(
                    total.at[before],
                    total.at[before],
                    total_send.at[0],
                    total_recv.at[before],
                    other,
                    y,
                ).wait_recv()
                now = state[...]
                state[...] = (
                    get_gain(total, before) * now
                    - mm(total[before, 0:C, :], now.astype(BF16))
                    + total[before, C : 2 * C, :].astype(F32)
                )

        entry = state[...]
        narrow = entry.astype(BF16)
        for j in range(NZ):
            here = prefix_g[j][0:1, :] * entry - mm(prefix_d[j], narrow) + prefix_c[j]
            give[j] = here.astype(BF16)
            for core in range(2):

                @pl.when((z != j) | (c != core))
                def _():
                    to_chip(j, core).start()

        take[z] = give[z]

    @pl.when(c == 1)
    def _():
        for h in range(HALF):
            to_other[h].wait_recv()

    for h in range(HEADS):

        @pl.when(jnp.logical_not(works) | (z != h))
        def _():
            remote(take.at[h], take.at[h], give_send.at[0], take_recv.at[h], other, y).wait_recv()

        @pl.when(c == 1)
        def _():
            now = take[h]
            here = (
                get_gain(sib, h) * now.astype(F32)
                - mm(sib[h, 0:C, :], now)
                + sib[h, C : 2 * C, :].astype(F32)
            )
            take[h] = here.astype(BF16)

        o = mm(read_ref[h].astype(BF16), take[h]) + local_ref[h]
        scale = lax.rsqrt(jnp.sum(o * o, axis=1, keepdims=True) * (1.0 / C) + 1e-6)
        normed[:, h * C : (h + 1) * C] = (o * scale * silu_ref[:, h * C : (h + 1) * C]).astype(BF16)

    def columns(to_y):
        return weight_ref[:, pl.ds(pl.multiple_of(to_y * OUT, OUT), OUT)]

    def to_row(step):
        return remote(
            part.at[step],
            parts.at[step],
            part_send.at[step],
            parts_recv.at[step],
            seq,
            lax.rem(y + step, NY),
        )

    for step in (2, 1, 3):
        part[step] = mm(normed[...], columns(lax.rem(y + step, NY))).astype(BF16)
        to_row(step).start()
    mine = mm(normed[...], columns(y))
    for step in (1, 3, 2):
        to_row(step).wait_recv()
        mine = mine + parts[step].astype(F32)
    out_ref[...] = mine.astype(BF16)

    for step in (2, 1, 3):
        to_row(step).wait_send()
    for h in range(HALF):
        to_other[h].wait_send()

    @pl.when(c == 0)
    def _():
        for h in range(HALF, HEADS):
            to_other[h].wait_send()

    for index in range(HALF):

        @pl.when(z != c * HALF + index)
        def _():
            to_chain(index).wait_send()

    @pl.when(works)
    def _():
        for step in range(1, NX):

            @pl.when(x + step < NX)
            def _():
                to_segment(step).wait_send()

        for j in range(NZ):
            for core in range(2):

                @pl.when((z != j) | (c != core))
                def _():
                    to_chip(j, core).wait_send()


def on_device(q, k, v, gate, decay, rate, init, gain, weight):
    vmem = pl.BlockSpec(memory_space=pltpu.VMEM)
    hbm = pl.BlockSpec(memory_space=pltpu.HBM)
    dma = pltpu.SemaphoreType.DMA
    return pl.pallas_call(
        kernel,
        out_shape=jax.ShapeDtypeStruct((C, OUT), BF16),
        in_specs=[hbm] * 9,
        out_specs=vmem,
        scratch_shapes=[
            pltpu.VMEM((C, KEYS * C), BF16),
            pltpu.VMEM((C, KEYS * C), BF16),
            pltpu.VMEM((C, HEADS * C), BF16),
            pltpu.VMEM((C, HEADS * C), BF16),
            pltpu.VMEM((HEADS, C), F32),
            pltpu.VMEM((HEADS, C), F32),
            pltpu.VMEM((HEADS, C, C), F32),
            pltpu.VMEM((1, C), F32),
            pltpu.VMEM((HEADS * C, NY * OUT), BF16),
            pltpu.VMEM((HEADS, C, 2 * C), BF16),
            pltpu.VMEM((HEADS, C, C), BF16),
            pltpu.VMEM((HEADS, C, C), F32),
            pltpu.VMEM((HEADS, C, C), F32),
            pltpu.VMEM((C, HEADS * C), F32),
            pltpu.VMEM((HEADS, MSG, C), BF16),
            pltpu.VMEM((HEADS, MSG, C), BF16),
            pltpu.VMEM((HALF, MSG, C), BF16),
            pltpu.VMEM((NZ, MSG, C), BF16),
            pltpu.VMEM((NX, MSG, C), BF16),
            pltpu.VMEM((NZ, C, C), BF16),
            pltpu.VMEM((NZ, C, C), F32),
            pltpu.VMEM((NZ, 8, C), F32),
            pltpu.VMEM((C, C), F32),
            pltpu.VMEM((NZ, C, C), BF16),
            pltpu.VMEM((HEADS, C, C), BF16),
            pltpu.VMEM((C, HEADS * C), BF16),
            pltpu.VMEM((NY, C, OUT), BF16),
            pltpu.VMEM((NY, C, OUT), BF16),
            dma((9,)),
            dma((HEADS,)),
            dma((HEADS,)),
            dma((HALF,)),
            dma((NZ,)),
            dma((NX,)),
            dma((NX,)),
            dma((2 * NZ,)),
            dma((HEADS,)),
            dma((NY,)),
            dma((NY,)),
        ],
        compiler_params=pltpu.CompilerParams(
            collective_id=0, has_side_effects=True, vmem_limit_bytes=62 * 2**20
        ),
        cost_estimate=pl.CostEstimate(
            flops=2 * 10**9, bytes_accessed=6 * 10**6, transcendentals=10**6
        ),
    )(q, k, v, gate, decay, rate, init, gain.reshape(1, C), weight)


def solution(mesh):
    return jax.shard_map(
        on_device,
        mesh=mesh,
        in_specs=(
            P("seq", "head"),
            P("seq", "head"),
            P("seq", "head"),
            P("seq", "head"),
            P("head", "seq"),
            P("head", "seq"),
            P("head", None, None),
            P(),
            P("head", None),
        ),
        out_specs=P("seq", "head"),
        check_vma=False,
    )
```

```python
import functools

import jax
import jax.numpy as jnp
from jax import lax
from jax.experimental import pallas as pl
from jax.experimental.pallas import tpu as pltpu
from jax.sharding import PartitionSpec as P

MESH = pl.DeviceIdType.MESH
F32 = jnp.float32
BF16 = jnp.bfloat16
HEADS = 8
KEYS = 4
C = 128
NX = 4
NZ = 8
NY = 4
HALF = HEADS // 2
MSG = 2 * C + 16
OUT = 512


def mm(a, b):
    return lax.dot_general(a, b, (((1,), (0,)), ((), ())), preferred_element_type=F32)


def mm_t(a, b):
    return lax.dot_general(a, b, (((1,), (1,)), ((), ())), preferred_element_type=F32)


def put_gain(ref, index, gain):
    wide = jnp.broadcast_to(gain, (8, C))
    high = wide.astype(BF16).astype(F32)
    ref[index, 2 * C :, :] = jnp.concatenate([high, wide - high], axis=0).astype(BF16)


def get_gain(ref, index):
    rows = ref[index, 2 * C :, :].astype(F32)
    return rows[0:1, :] + rows[8:9, :]


def kernel(
    q_hbm,
    k_hbm,
    v_hbm,
    gate_hbm,
    decay_hbm,
    rate_hbm,
    init_hbm,
    gain_hbm,
    weight_hbm,
    out_ref,
    q_ref,
    k_ref,
    v_ref,
    gate_ref,
    decay_ref,
    rate_ref,
    init_ref,
    gain_ref,
    weight_ref,
    wu_ref,
    score_ref,
    read_ref,
    local_ref,
    silu_ref,
    own,
    sib,
    comb,
    chain,
    total,
    prefix_d,
    prefix_c,
    prefix_g,
    state,
    give,
    take,
    normed,
    far,
    relay,
    part,
    parts,
    load_sem,
    sib_send,
    sib_recv,
    comb_send,
    chain_recv,
    total_send,
    total_recv,
    give_send,
    take_recv,
    forward_send,
    part_send,
    parts_recv,
):
    seq, y = lax.axis_index("seq"), lax.axis_index("head")
    x, z, c = seq // 16, lax.rem(seq // 2, NZ), lax.rem(seq, 2)
    base = x * 16
    other = base + z * 2 + (1 - c)

    def remote(src, dst, send, recv, to_seq, to_y):
        return pltpu.make_async_remote_copy(
            src_ref=src,
            dst_ref=dst,
            send_sem=send,
            recv_sem=recv,
            device_id=(to_seq, to_y),
            device_id_type=MESH,
        )

    pairs = (
        (decay_hbm, decay_ref),
        (rate_hbm, rate_ref),
        (k_hbm, k_ref),
        (q_hbm, q_ref),
        (v_hbm, v_ref),
        (gate_hbm, gate_ref),
        (gain_hbm, gain_ref),
        (init_hbm, init_ref),
        (weight_hbm, weight_ref),
    )
    loads = [
        pltpu.make_async_copy(src, dst, load_sem.at[i]) for i, (src, dst) in enumerate(pairs)
    ]
    for load in loads:
        load.start()
    barrier = pltpu.get_barrier_semaphore()
    for step in range(1, 16):
        pl.semaphore_signal(
            barrier, inc=1, device_id=(base + lax.rem(z * 2 + c + step, 16), y), device_id_type=MESH
        )
    for step in range(1, NX):
        pl.semaphore_signal(
            barrier, inc=1, device_id=(lax.rem(seq + 16 * step, 64), y), device_id_type=MESH
        )
    for step in range(1, NY):
        pl.semaphore_signal(
            barrier, inc=1, device_id=(seq, lax.rem(y + step, NY)), device_id_type=MESH
        )

    rows = lax.broadcasted_iota(jnp.int32, (C, C), 0)
    cols = lax.broadcasted_iota(jnp.int32, (C, C), 1)
    apart = rows ^ cols
    strict = rows > cols
    within = rows >= cols
    diagonal = (rows == cols).astype(F32)
    upto = (rows <= cols).astype(BF16)
    for load in loads[0:5]:
        load.wait()
    logs = jnp.log(decay_ref[...])
    rates = rate_ref[...]
    high = logs.astype(BF16)
    rest = logs - high.astype(F32)
    middle = rest.astype(BF16)
    low = (rest - middle.astype(F32)).astype(BF16)
    cum = mm(high, upto) + (mm(middle, upto) + mm(low, upto))
    tall = jnp.concatenate([cum, rates, jnp.zeros((C - 2 * HEADS, C), F32)], axis=0).T
    ends = [cum[h : h + 1, C - 1 : C] for h in range(HEADS)]

    lower, inverse, row_keys, col_keys = [], [], [], []
    for kh in range(KEYS):
        keys = k_ref[:, kh * C : (kh + 1) * C]
        asks = q_ref[:, kh * C : (kh + 1) * C]
        inner = mm_t(keys, keys)
        cross = mm_t(asks, keys)
        squares = inner * diagonal
        row_key = lax.rsqrt(jnp.sum(squares, axis=0, keepdims=True) + 1e-6)
        col_key = lax.rsqrt(jnp.sum(squares, axis=1, keepdims=True) + 1e-6)
        wide_asks = asks.astype(F32)
        col_ask = lax.rsqrt(jnp.sum(wide_asks * wide_asks, axis=1, keepdims=True) + 1e-6)
        col_ask = col_ask * (C**-0.5)
        row_keys.append(row_key)
        col_keys.append(col_key)
        for h in (2 * kh, 2 * kh + 1):
            cum_col = tall[:, h : h + 1]
            rate_col = tall[:, HEADS + h : HEADS + h + 1]
            fade = jnp.exp(jnp.where(within, cum_col - cum[h : h + 1, :], 0.0))
            fade = fade * row_key
            low_part = jnp.where(strict, inner * fade * (rate_col * col_key), 0.0).astype(BF16)
            lower.append(low_part)
            score_ref[h] = jnp.where(within, cross * fade * col_ask, 0.0).astype(BF16)
            read_ref[h] = wide_asks * (col_ask * jnp.exp(cum_col))
            inverse.append(jnp.where(apart == 1, -low_part.astype(F32), diagonal).astype(BF16))
    size = 2
    while size < C:
        mask = ((apart >= size) & (apart < 2 * size)).astype(BF16)
        firsts = [mm(inverse[h], lower[h] * mask).astype(BF16) for h in range(HEADS)]
        inverse = [inverse[h] - mm(firsts[h], inverse[h]).astype(BF16) for h in range(HEADS)]
        size *= 2
    for kh in range(KEYS):
        keys = k_ref[:, kh * C : (kh + 1) * C]
        keys_t = keys.astype(F32).T.astype(BF16)
        for h in (2 * kh, 2 * kh + 1):
            wide = inverse[h].astype(F32)
            rate_row = rates[h : h + 1, :]
            cum_row = cum[h : h + 1, :]
            w_part = mm((wide * (rate_row * jnp.exp(cum_row) * row_keys[kh])).astype(BF16), keys)
            u_part = mm((wide * rate_row).astype(BF16), v_ref[:, h * C : (h + 1) * C])
            both = jnp.concatenate([w_part, u_part], axis=1)
            wu_ref[h] = both.astype(BF16)
            fade_col = col_keys[kh] * jnp.exp(ends[h] - tall[:, h : h + 1])
            maps = mm(keys_t, (both * fade_col).astype(BF16))
            own[h, 0:C, :] = maps[:, 0:C].astype(BF16)
            own[h, C : 2 * C, :] = maps[:, C:].astype(BF16)
            put_gain(own, h, jnp.exp(ends[h]))

    pl.semaphore_wait(barrier, 15 + NX - 1 + NY - 1)

    to_other = [
        remote(own.at[h], sib.at[h], sib_send.at[h], sib_recv.at[h], other, y)
        for h in range(HEADS)
    ]

    @pl.when(c == 0)
    def _():
        for h in range(HALF, HEADS):
            to_other[h].start()

    for h in range(HALF):
        to_other[h].start()

    def joined(index):
        h = c * HALF + index
        remote(own.at[h], sib.at[h], sib_send.at[h], sib_recv.at[h], other, y).wait_recv()
        mine, theirs = own[h, 0 : 2 * C, :], sib[h, 0 : 2 * C, :]
        my_gain, their_gain = get_gain(own, h), get_gain(sib, h)
        first = c == 0
        early = jnp.where(first, mine.astype(F32), theirs.astype(F32))
        late = jnp.where(first, theirs.astype(F32), mine.astype(F32))
        early_gain = jnp.where(first, my_gain, their_gain)
        late_gain = jnp.where(first, their_gain, my_gain)
        late_map = late[0:C].astype(BF16)
        pair = jnp.concatenate([early[0:C], early[C:]], axis=1).astype(BF16)
        moved = mm(late_map, pair)
        comb[index, 0:C, :] = (
            late_gain * early[0:C] + early_gain * late[0:C] - moved[:, 0:C]
        ).astype(BF16)
        comb[index, C : 2 * C, :] = (late_gain * early[C:] + late[C:] - moved[:, C:]).astype(BF16)
        put_gain(comb, index, early_gain * late_gain)

    def to_chain(index):
        h = c * HALF + index
        return remote(
            comb.at[index],
            chain.at[z],
            comb_send.at[index],
            chain_recv.at[z],
            base + h * 2 + c,
            y,
        )

    for index in range(HALF):
        joined(index)

        @pl.when(z != c * HALF + index)
        def _():
            to_chain(index).start()

        @pl.when(z == c * HALF + index)
        def _():
            chain[z] = comb[index]

    for h in range(HEADS):
        pair = mm(score_ref[h], wu_ref[h])
        read_ref[h] = read_ref[h] - pair[:, 0:C]
        local_ref[h] = pair[:, C:]
    @pl.when(c == 1)
    def _():
        for h in range(HALF):
            to_other[h].wait_recv()
        for h in range(HEADS):
            now = read_ref[h]
            narrow = now.astype(BF16)
            read_ref[h] = get_gain(sib, h) * now - mm(narrow, sib[h, 0:C, :])
            local_ref[h] = local_ref[h] + mm(narrow, sib[h, C : 2 * C, :])

    for load in loads[5:]:
        load.wait()
    gate = gate_ref[...].astype(F32)
    gains = jnp.concatenate([gain_ref[...]] * HEADS, axis=1)
    silu_ref[...] = gate / (1.0 + jnp.exp(-gate)) * gains

    works = z // HALF == c

    def to_segment(step):
        return remote(
            total.at[x],
            total.at[x],
            total_send.at[step],
            total_recv.at[x],
            lax.rem(seq + 16 * step, 64),
            y,
        )

    def to_chip(j):
        return remote(
            give.at[j], take.at[z], give_send.at[j], take_recv.at[z], base + j * 2 + c, y
        )

    def to_sibling(index):
        h = c * HALF + index
        return remote(take.at[h], take.at[h], forward_send.at[index], take_recv.at[h], other, y)

    @pl.when(works)
    def _():
        d_now = jnp.zeros((C, C), F32)
        c_now = jnp.zeros((C, C), F32)
        g_now = jnp.ones((1, C), F32)
        for j in range(NZ):

            @pl.when(z != j)
            def _():
                remote(
                    chain.at[j], chain.at[j], comb_send.at[0], chain_recv.at[j], other, y
                ).wait_recv()

            prefix_d[j] = d_now.astype(BF16)
            prefix_c[j] = c_now
            prefix_g[j] = jnp.broadcast_to(g_now, (8, C))
            step_map = chain[j, 0:C, :]
            step_bias = chain[j, C : 2 * C, :].astype(F32)
            gain = get_gain(chain, j)
            wide_map = step_map.astype(F32)
            if j == 0:
                d_now, c_now = wide_map, step_bias
            else:
                moved = mm(step_map, jnp.concatenate([d_now, c_now], axis=1).astype(BF16))
                d_now = gain * d_now + g_now * wide_map - moved[:, 0:C]
                c_now = gain * c_now + step_bias - moved[:, C:]
            g_now = g_now * gain
        total[x, 0:C, :] = d_now.astype(BF16)
        total[x, C : 2 * C, :] = c_now.astype(BF16)
        put_gain(total, x, g_now)
        for step in range(1, NX):

            @pl.when(x + step < NX)
            def _():
                to_segment(step).start()

        state[...] = init_ref[z]
        for before in range(NX - 1):

            @pl.when(before < x)
            def _():
                remote(
                    total.at[before],
                    total.at[before],
                    total_send.at[0],
                    total_recv.at[before],
                    other,
                    y,
                ).wait_recv()
                now = state[...]
                state[...] = (
                    get_gain(total, before) * now
                    - mm(total[before, 0:C, :], now.astype(BF16))
                    + total[before, C : 2 * C, :].astype(F32)
                )

        entry = state[...]
        narrow = entry.astype(BF16)
        for j in range(NZ):
            here = prefix_g[j][0:1, :] * entry - mm(prefix_d[j], narrow) + prefix_c[j]
            give[j] = here.astype(BF16)

            @pl.when(z != j)
            def _():
                to_chip(j).start()

        take[z] = give[z]

    for index in range(HALF):
        h = c * HALF + index

        @pl.when(z != h)
        def _():
            remote(take.at[h], take.at[h], give_send.at[0], take_recv.at[h], other, y).wait_recv()

        to_sibling(index).start()
    for index in range(HALF):
        h = (1 - c) * HALF + index
        remote(take.at[h], take.at[h], give_send.at[0], take_recv.at[h], other, y).wait_recv()
    for h in range(HEADS):
        o = mm(read_ref[h].astype(BF16), take[h]) + local_ref[h]
        scale = lax.rsqrt(jnp.sum(o * o, axis=1, keepdims=True) * (1.0 / C) + 1e-6)
        normed[:, h * C : (h + 1) * C] = (o * scale * silu_ref[:, h * C : (h + 1) * C]).astype(BF16)

    def columns(to_y):
        return weight_ref[:, pl.ds(pl.multiple_of(to_y * OUT, OUT), OUT)]

    above, below = lax.rem(y + 1, NY), lax.rem(y + NY - 1, NY)
    upper, lower_half = pl.ds(0, C // 2), pl.ds(C // 2, C // 2)

    def row_copy(src, dst, i, to_y):
        return remote(src, dst, part_send.at[i], parts_recv.at[i], seq, to_y)

    copies = (
        row_copy(far.at[upper], relay.at[0], 0, above),
        row_copy(far.at[lower_half], relay.at[1], 1, below),
        row_copy(part.at[0, lower_half], parts.at[0, lower_half], 2, above),
        row_copy(part.at[1, upper], parts.at[1, upper], 3, below),
        row_copy(part.at[0, upper], parts.at[0, upper], 4, above),
        row_copy(part.at[1, lower_half], parts.at[1, lower_half], 5, below),
    )
    far[...] = mm(normed[...], columns(lax.rem(y + 2, NY))).astype(BF16)
    copies[0].start()
    copies[1].start()
    rising = mm(normed[...], columns(above))
    part[0, C // 2 :, :] = rising[C // 2 :].astype(BF16)
    copies[2].start()
    falling = mm(normed[...], columns(below))
    part[1, 0 : C // 2, :] = falling[0 : C // 2].astype(BF16)
    copies[3].start()
    copies[0].wait_recv()
    part[0, 0 : C // 2, :] = (rising[0 : C // 2] + relay[0].astype(F32)).astype(BF16)
    copies[4].start()
    copies[1].wait_recv()
    part[1, C // 2 :, :] = (falling[C // 2 :] + relay[1].astype(F32)).astype(BF16)
    copies[5].start()
    mine = mm(normed[...], columns(y))
    for i in (2, 3, 4, 5):
        copies[i].wait_recv()
    out_ref[...] = (mine + parts[0].astype(F32) + parts[1].astype(F32)).astype(BF16)

    for copy in copies:
        copy.wait_send()
    for index in range(HALF):
        to_sibling(index).wait_send()
    for h in range(HALF):
        to_other[h].wait_send()

    @pl.when(c == 0)
    def _():
        for h in range(HALF, HEADS):
            to_other[h].wait_send()

    for index in range(HALF):

        @pl.when(z != c * HALF + index)
        def _():
            to_chain(index).wait_send()

    @pl.when(works)
    def _():
        for step in range(1, NX):

            @pl.when(x + step < NX)
            def _():
                to_segment(step).wait_send()

        for j in range(NZ):

            @pl.when(z != j)
            def _():
                to_chip(j).wait_send()


def on_device(q, k, v, gate, decay, rate, init, gain, weight):
    vmem = pl.BlockSpec(memory_space=pltpu.VMEM)
    hbm = pl.BlockSpec(memory_space=pltpu.HBM)
    dma = pltpu.SemaphoreType.DMA
    return pl.pallas_call(
        kernel,
        out_shape=jax.ShapeDtypeStruct((C, OUT), BF16),
        in_specs=[hbm] * 9,
        out_specs=vmem,
        scratch_shapes=[
            pltpu.VMEM((C, KEYS * C), BF16),
            pltpu.VMEM((C, KEYS * C), BF16),
            pltpu.VMEM((C, HEADS * C), BF16),
            pltpu.VMEM((C, HEADS * C), BF16),
            pltpu.VMEM((HEADS, C), F32),
            pltpu.VMEM((HEADS, C), F32),
            pltpu.VMEM((HEADS, C, C), F32),
            pltpu.VMEM((1, C), F32),
            pltpu.VMEM((HEADS * C, NY * OUT), BF16),
            pltpu.VMEM((HEADS, C, 2 * C), BF16),
            pltpu.VMEM((HEADS, C, C), BF16),
            pltpu.VMEM((HEADS, C, C), F32),
            pltpu.VMEM((HEADS, C, C), F32),
            pltpu.VMEM((C, HEADS * C), F32),
            pltpu.VMEM((HEADS, MSG, C), BF16),
            pltpu.VMEM((HEADS, MSG, C), BF16),
            pltpu.VMEM((HALF, MSG, C), BF16),
            pltpu.VMEM((NZ, MSG, C), BF16),
            pltpu.VMEM((NX, MSG, C), BF16),
            pltpu.VMEM((NZ, C, C), BF16),
            pltpu.VMEM((NZ, C, C), F32),
            pltpu.VMEM((NZ, 8, C), F32),
            pltpu.VMEM((C, C), F32),
            pltpu.VMEM((NZ, C, C), BF16),
            pltpu.VMEM((HEADS, C, C), BF16),
            pltpu.VMEM((C, HEADS * C), BF16),
            pltpu.VMEM((C, OUT), BF16),
            pltpu.VMEM((2, C // 2, OUT), BF16),
            pltpu.VMEM((2, C, OUT), BF16),
            pltpu.VMEM((2, C, OUT), BF16),
            dma((9,)),
            dma((HEADS,)),
            dma((HEADS,)),
            dma((HALF,)),
            dma((NZ,)),
            dma((NX,)),
            dma((NX,)),
            dma((NZ,)),
            dma((HEADS,)),
            dma((HALF,)),
            dma((6,)),
            dma((6,)),
        ],
        compiler_params=pltpu.CompilerParams(
            collective_id=0, has_side_effects=True, vmem_limit_bytes=62 * 2**20
        ),
        cost_estimate=pl.CostEstimate(
            flops=2 * 10**9, bytes_accessed=6 * 10**6, transcendentals=10**6
        ),
    )(q, k, v, gate, decay, rate, init, gain.reshape(1, C), weight)


def solution(mesh):
    return jax.shard_map(
        on_device,
        mesh=mesh,
        in_specs=(
            P("seq", "head"),
            P("seq", "head"),
            P("seq", "head"),
            P("seq", "head"),
            P("head", "seq"),
            P("head", "seq"),
            P("head", None, None),
            P(),
            P("head", None),
        ),
        out_specs=P("seq", "head"),
        check_vma=False,
    )
```

```python
import functools

import jax
import jax.numpy as jnp
from jax import lax
from jax.experimental import pallas as pl
from jax.experimental.pallas import tpu as pltpu
from jax.sharding import PartitionSpec as P

MESH = pl.DeviceIdType.MESH
F32 = jnp.float32
BF16 = jnp.bfloat16
HEADS = 8
KEYS = 4
C = 128
NX = 4
NZ = 8
NY = 4
HALF = HEADS // 2
MSG = 2 * C + 16
OUT = 512
PIECE = 256


def mm(a, b):
    return lax.dot_general(a, b, (((1,), (0,)), ((), ())), preferred_element_type=F32)


def mm_t(a, b):
    return lax.dot_general(a, b, (((1,), (1,)), ((), ())), preferred_element_type=F32)


def put_gain(ref, index, gain):
    wide = jnp.broadcast_to(gain, (8, C))
    high = wide.astype(BF16).astype(F32)
    ref[index, 2 * C :, :] = jnp.concatenate([high, wide - high], axis=0).astype(BF16)


def get_gain(ref, index):
    rows = ref[index, 2 * C :, :].astype(F32)
    return rows[0:1, :] + rows[8:9, :]


def kernel(
    q_hbm,
    k_hbm,
    v_hbm,
    gate_hbm,
    decay_hbm,
    rate_hbm,
    init_hbm,
    gain_hbm,
    weight_hbm,
    out_ref,
    q_ref,
    k_ref,
    v_ref,
    gate_ref,
    decay_ref,
    rate_ref,
    init_ref,
    gain_ref,
    weight_ref,
    wu_ref,
    fade_ref,
    read_ref,
    local_ref,
    silu_ref,
    pair,
    comb,
    chain,
    total,
    prefix_d,
    prefix_c,
    prefix_g,
    state,
    give,
    take,
    normed,
    far,
    relay,
    plain,
    plains,
    part,
    parts,
    load_sem,
    sib_send,
    sib_recv,
    comb_send,
    chain_recv,
    total_send,
    total_recv,
    give_send,
    take_recv,
    forward_send,
    part_send,
    parts_recv,
):
    seq, y = lax.axis_index("seq"), lax.axis_index("head")
    x, z, c = seq // 16, lax.rem(seq // 2, NZ), lax.rem(seq, 2)
    base = x * 16
    other = base + z * 2 + (1 - c)

    def remote(src, dst, send, recv, to_seq, to_y):
        return pltpu.make_async_remote_copy(
            src_ref=src,
            dst_ref=dst,
            send_sem=send,
            recv_sem=recv,
            device_id=(to_seq, to_y),
            device_id_type=MESH,
        )

    pairs = (
        (decay_hbm, decay_ref),
        (rate_hbm, rate_ref),
        (k_hbm, k_ref),
        (v_hbm, v_ref),
        (q_hbm, q_ref),
        (gate_hbm, gate_ref),
        (gain_hbm, gain_ref),
        (init_hbm, init_ref),
        (weight_hbm, weight_ref),
    )
    loads = [
        pltpu.make_async_copy(src, dst, load_sem.at[i]) for i, (src, dst) in enumerate(pairs)
    ]
    for load in loads[0:4]:
        load.start()
    barrier = pltpu.get_barrier_semaphore()
    for step in range(1, 16):
        pl.semaphore_signal(
            barrier, inc=1, device_id=(base + lax.rem(z * 2 + c + step, 16), y), device_id_type=MESH
        )
    for step in range(1, NX):
        pl.semaphore_signal(
            barrier, inc=1, device_id=(lax.rem(seq + 16 * step, 64), y), device_id_type=MESH
        )
    for step in range(1, NY):
        pl.semaphore_signal(
            barrier, inc=1, device_id=(seq, lax.rem(y + step, NY)), device_id_type=MESH
        )

    rows = lax.broadcasted_iota(jnp.int32, (C, C), 0)
    cols = lax.broadcasted_iota(jnp.int32, (C, C), 1)
    apart = rows ^ cols
    strict = rows > cols
    within = rows >= cols
    diagonal = (rows == cols).astype(F32)
    upto = (rows <= cols).astype(BF16)
    for load in loads[0:3]:
        load.wait()
    logs = jnp.log(decay_ref[...])
    rates = rate_ref[...]
    high = logs.astype(BF16)
    rest = logs - high.astype(F32)
    middle = rest.astype(BF16)
    low = (rest - middle.astype(F32)).astype(BF16)
    cum = mm(high, upto) + (mm(middle, upto) + mm(low, upto))
    tall = jnp.concatenate([cum, rates, jnp.zeros((C - 2 * HEADS, C), F32)], axis=0).T
    ends = [cum[h : h + 1, C - 1 : C] for h in range(HEADS)]

    lower, inverse, row_keys, col_keys = [], [], [], []
    for kh in range(KEYS):
        keys = k_ref[:, kh * C : (kh + 1) * C]
        inner = mm_t(keys, keys)
        squares = inner * diagonal
        row_key = lax.rsqrt(jnp.sum(squares, axis=0, keepdims=True) + 1e-6)
        col_key = lax.rsqrt(jnp.sum(squares, axis=1, keepdims=True) + 1e-6)
        row_keys.append(row_key)
        col_keys.append(col_key)
        for h in (2 * kh, 2 * kh + 1):
            cum_col = tall[:, h : h + 1]
            rate_col = tall[:, HEADS + h : HEADS + h + 1]
            fade = jnp.exp(jnp.where(within, cum_col - cum[h : h + 1, :], 0.0))
            fade = jnp.where(within, fade * row_key, 0.0)
            fade_ref[h] = fade
            low_part = jnp.where(strict, inner * fade * (rate_col * col_key), 0.0).astype(BF16)
            lower.append(low_part)
            inverse.append(jnp.where(apart == 1, -low_part.astype(F32), diagonal).astype(BF16))
    loads[3].wait()
    for load in loads[4:]:
        load.start()
    size = 2
    while size < C:
        mask = ((apart >= size) & (apart < 2 * size)).astype(BF16)
        firsts = [mm(inverse[h], lower[h] * mask).astype(BF16) for h in range(HEADS)]
        inverse = [inverse[h] - mm(firsts[h], inverse[h]).astype(BF16) for h in range(HEADS)]
        size *= 2
    for kh in range(KEYS):
        keys = k_ref[:, kh * C : (kh + 1) * C]
        keys_t = keys.astype(F32).T.astype(BF16)
        for h in (2 * kh, 2 * kh + 1):
            wide = inverse[h].astype(F32)
            rate_row = rates[h : h + 1, :]
            cum_row = cum[h : h + 1, :]
            w_part = mm((wide * (rate_row * jnp.exp(cum_row) * row_keys[kh])).astype(BF16), keys)
            u_part = mm((wide * rate_row).astype(BF16), v_ref[:, h * C : (h + 1) * C])
            both = jnp.concatenate([w_part, u_part], axis=1)
            wu_ref[h] = both.astype(BF16)
            fade_col = col_keys[kh] * jnp.exp(ends[h] - tall[:, h : h + 1])
            maps = mm(keys_t, (both * fade_col).astype(BF16))
            pair[c, h, 0:C, :] = maps[:, 0:C].astype(BF16)
            pair[c, h, C : 2 * C, :] = maps[:, C:].astype(BF16)
            put_gain(pair.at[c], h, jnp.exp(ends[h]))

    pl.semaphore_wait(barrier, 15 + NX - 1 + NY - 1)

    def to_other(h):
        return remote(
            pair.at[c, h], pair.at[c, h], sib_send.at[h], sib_recv.at[h], other, y
        )

    def from_other(h):
        return remote(
            pair.at[1 - c, h], pair.at[1 - c, h], sib_send.at[h], sib_recv.at[h], other, y
        )

    for index in range(HALF):
        to_other((1 - c) * HALF + index).start()

    @pl.when(c == 0)
    def _():
        for h in range(HALF):
            to_other(h).start()

    def joined(index):
        h = c * HALF + index
        early, late = pair.at[0], pair.at[1]
        early_gain, late_gain = get_gain(early, h), get_gain(late, h)
        early_map, late_map = early[h, 0:C, :], late[h, 0:C, :]
        early_bias, late_bias = early[h, C : 2 * C, :], late[h, C : 2 * C, :]
        moved = mm(late_map, jnp.concatenate([early_map, early_bias], axis=1))
        comb[index, 0:C, :] = (
            late_gain * early_map.astype(F32) + early_gain * late_map.astype(F32) - moved[:, 0:C]
        ).astype(BF16)
        comb[index, C : 2 * C, :] = (
            late_gain * early_bias.astype(F32) + late_bias.astype(F32) - moved[:, C:]
        ).astype(BF16)
        put_gain(comb, index, early_gain * late_gain)

    def to_chain(index):
        h = c * HALF + index
        return remote(
            comb.at[index],
            chain.at[z],
            comb_send.at[index],
            chain_recv.at[z],
            base + h * 2 + c,
            y,
        )

    for group in (0, 2):
        for index in (group, group + 1):
            from_other(c * HALF + index).wait_recv()
        for index in (group, group + 1):
            joined(index)
        for index in (group, group + 1):

            @pl.when(z != c * HALF + index)
            def _():
                to_chain(index).start()

            @pl.when(z == c * HALF + index)
            def _():
                chain[z] = comb[index]

    loads[4].wait()
    for kh in range(KEYS):
        keys = k_ref[:, kh * C : (kh + 1) * C]
        asks = q_ref[:, kh * C : (kh + 1) * C]
        wide_asks = asks.astype(F32)
        col_ask = lax.rsqrt(jnp.sum(wide_asks * wide_asks, axis=1, keepdims=True) + 1e-6)
        col_ask = col_ask * (C**-0.5)
        cross = mm_t(asks, keys) * col_ask
        for h in (2 * kh, 2 * kh + 1):
            both = mm((cross * fade_ref[h]).astype(BF16), wu_ref[h])
            read_ref[h] = wide_asks * (col_ask * jnp.exp(tall[:, h : h + 1])) - both[:, 0:C]
            local_ref[h] = both[:, C:]

    @pl.when(c == 1)
    def _():
        for h in range(HALF):
            from_other(h).wait_recv()
        for h in range(HEADS):
            now = read_ref[h]
            narrow = now.astype(BF16)
            read_ref[h] = get_gain(pair.at[0], h) * now - mm(narrow, pair[0, h, 0:C, :])
            local_ref[h] = local_ref[h] + mm(narrow, pair[0, h, C : 2 * C, :])

    for load in loads[5:]:
        load.wait()
    gate = gate_ref[...].astype(F32)
    gains = jnp.concatenate([gain_ref[...]] * HEADS, axis=1)
    silu_ref[...] = gate / (1.0 + jnp.exp(-gate)) * gains

    works = z // HALF == c

    def to_segment(step):
        return remote(
            total.at[x],
            total.at[x],
            total_send.at[step],
            total_recv.at[x],
            lax.rem(seq + 16 * step, 64),
            y,
        )

    def to_chip(j):
        return remote(
            give.at[j], take.at[z], give_send.at[j], take_recv.at[z], base + j * 2 + c, y
        )

    def to_sibling(index):
        h = c * HALF + index
        return remote(take.at[h], take.at[h], forward_send.at[index], take_recv.at[h], other, y)

    @pl.when(works)
    def _():
        d_now = jnp.zeros((C, C), F32)
        c_now = jnp.zeros((C, C), F32)
        g_now = jnp.ones((1, C), F32)
        for j in range(NZ):

            @pl.when(z != j)
            def _():
                remote(
                    chain.at[j], chain.at[j], comb_send.at[0], chain_recv.at[j], other, y
                ).wait_recv()

            prefix_d[j * C : (j + 1) * C, :] = d_now.astype(BF16)
            prefix_c[j * C : (j + 1) * C, :] = c_now
            prefix_g[j] = jnp.broadcast_to(g_now, (8, C))
            step_map = chain[j, 0:C, :]
            step_bias = chain[j, C : 2 * C, :].astype(F32)
            gain = get_gain(chain, j)
            wide_map = step_map.astype(F32)
            if j == 0:
                d_now, c_now = wide_map, step_bias
            else:
                moved = mm(step_map, jnp.concatenate([d_now, c_now], axis=1).astype(BF16))
                d_now = gain * d_now + g_now * wide_map - moved[:, 0:C]
                c_now = gain * c_now + step_bias - moved[:, C:]
            g_now = g_now * gain
        total[x, 0:C, :] = d_now.astype(BF16)
        total[x, C : 2 * C, :] = c_now.astype(BF16)
        put_gain(total, x, g_now)
        for step in (2, 1, 3):

            @pl.when(x + step < NX)
            def _():
                to_segment(step).start()

        state[...] = init_ref[z]
        for before in range(NX - 1):

            @pl.when(before < x)
            def _():
                remote(
                    total.at[before],
                    total.at[before],
                    total_send.at[0],
                    total_recv.at[before],
                    other,
                    y,
                ).wait_recv()
                now = state[...]
                state[...] = (
                    get_gain(total, before) * now
                    - mm(total[before, 0:C, :], now.astype(BF16))
                    + total[before, C : 2 * C, :].astype(F32)
                )

        entry = state[...]
        narrow = entry.astype(BF16)
        moved = mm(prefix_d[...], narrow)
        for j in range(NZ):
            span = slice(j * C, (j + 1) * C)
            here = prefix_g[j][0:1, :] * entry - moved[span] + prefix_c[span]
            give[j] = here.astype(BF16)
        for j in range(NZ):

            @pl.when(z != j)
            def _():
                to_chip(j).start()

        take[z] = give[z]

    for index in range(HALF):
        h = c * HALF + index

        @pl.when(z != h)
        def _():
            remote(take.at[h], take.at[h], give_send.at[0], take_recv.at[h], other, y).wait_recv()

        to_sibling(index).start()
    for index in range(HALF):
        h = (1 - c) * HALF + index
        remote(take.at[h], take.at[h], give_send.at[0], take_recv.at[h], other, y).wait_recv()
    for h in range(HEADS):
        o = mm(read_ref[h].astype(BF16), take[h]) + local_ref[h]
        scale = lax.rsqrt(jnp.sum(o * o, axis=1, keepdims=True) * (1.0 / C) + 1e-6)
        normed[:, h * C : (h + 1) * C] = (o * scale * silu_ref[:, h * C : (h + 1) * C]).astype(BF16)

    def columns(to_y, start, size):
        return weight_ref[:, pl.ds(pl.multiple_of(to_y * OUT + start, PIECE), size)]

    above, below = lax.rem(y + 1, NY), lax.rem(y + NY - 1, NY)
    half = (pl.ds(0, C // 2), pl.ds(C // 2, C // 2))

    def row_copy(src, dst, i, to_y):
        return remote(src, dst, part_send.at[i], parts_recv.at[i], seq, to_y)

    relays, sums, directs = [], [], []
    for way, to_y in enumerate((above, below)):
        directs.append(row_copy(plain.at[way], plains.at[way], way, to_y))
        for n in range(2):
            relays.append(
                row_copy(far.at[n, half[way]], relay.at[way, n], 2 + 2 * way + n, to_y)
            )
            sums.append(
                row_copy(part.at[way, n], parts.at[way, n], 6 + 2 * way + n, to_y)
            )
    for n in range(2):
        far[n] = mm(normed[...], columns(lax.rem(y + 2, NY), n * PIECE, PIECE)).astype(BF16)
        relays[n].start()
        relays[2 + n].start()
    totals = []
    for way, to_y in enumerate((above, below)):
        whole = mm(normed[...], columns(to_y, 0, OUT))
        totals.append(whole)
        first = C // 2 if way == 0 else 0
        for n in range(2):
            plain[way, n] = whole[
                first : first + C // 2, n * PIECE : (n + 1) * PIECE
            ].astype(BF16)
        directs[way].start()
    mine = mm(normed[...], columns(y, 0, OUT))
    for n in range(2):
        for way in range(2):
            first = 0 if way == 0 else C // 2
            relays[2 * way + n].wait_recv()
            term = totals[way][first : first + C // 2, n * PIECE : (n + 1) * PIECE]
            part[way, n] = (term + relay[way, n].astype(F32)).astype(BF16)
            sums[2 * way + n].start()
    for copy in directs:
        copy.wait_recv()
    for n in range(2):
        for way in range(2):
            sums[2 * way + n].wait_recv()
        span = slice(n * PIECE, (n + 1) * PIECE)
        out_ref[0 : C // 2, span] = (
            mine[0 : C // 2, span] + parts[0, n].astype(F32) + plains[1, n].astype(F32)
        ).astype(BF16)
        out_ref[C // 2 :, span] = (
            mine[C // 2 :, span] + plains[0, n].astype(F32) + parts[1, n].astype(F32)
        ).astype(BF16)

    for copy in relays + directs + sums:
        copy.wait_send()
    for index in range(HALF):
        to_sibling(index).wait_send()
    for index in range(HALF):
        to_other((1 - c) * HALF + index).wait_send()

    @pl.when(c == 0)
    def _():
        for h in range(HALF):
            to_other(h).wait_send()

    for index in range(HALF):

        @pl.when(z != c * HALF + index)
        def _():
            to_chain(index).wait_send()

    @pl.when(works)
    def _():
        for step in range(1, NX):

            @pl.when(x + step < NX)
            def _():
                to_segment(step).wait_send()

        for away in range(1, NZ):
            to_chip(lax.rem(z + away, NZ)).wait_send()


def on_device(q, k, v, gate, decay, rate, init, gain, weight):
    vmem = pl.BlockSpec(memory_space=pltpu.VMEM)
    hbm = pl.BlockSpec(memory_space=pltpu.HBM)
    dma = pltpu.SemaphoreType.DMA
    return pl.pallas_call(
        kernel,
        out_shape=jax.ShapeDtypeStruct((C, OUT), BF16),
        in_specs=[hbm] * 9,
        out_specs=vmem,
        scratch_shapes=[
            pltpu.VMEM((C, KEYS * C), BF16),
            pltpu.VMEM((C, KEYS * C), BF16),
            pltpu.VMEM((C, HEADS * C), BF16),
            pltpu.VMEM((C, HEADS * C), BF16),
            pltpu.VMEM((HEADS, C), F32),
            pltpu.VMEM((HEADS, C), F32),
            pltpu.VMEM((HEADS, C, C), F32),
            pltpu.VMEM((1, C), F32),
            pltpu.VMEM((HEADS * C, NY * OUT), BF16),
            pltpu.VMEM((HEADS, C, 2 * C), BF16),
            pltpu.VMEM((HEADS, C, C), F32),
            pltpu.VMEM((HEADS, C, C), F32),
            pltpu.VMEM((HEADS, C, C), F32),
            pltpu.VMEM((C, HEADS * C), F32),
            pltpu.VMEM((2, HEADS, MSG, C), BF16),
            pltpu.VMEM((HALF, MSG, C), BF16),
            pltpu.VMEM((NZ, MSG, C), BF16),
            pltpu.VMEM((NX, MSG, C), BF16),
            pltpu.VMEM((NZ * C, C), BF16),
            pltpu.VMEM((NZ * C, C), F32),
            pltpu.VMEM((NZ, 8, C), F32),
            pltpu.VMEM((C, C), F32),
            pltpu.VMEM((NZ, C, C), BF16),
            pltpu.VMEM((HEADS, C, C), BF16),
            pltpu.VMEM((C, HEADS * C), BF16),
            pltpu.VMEM((2, C, PIECE), BF16),
            pltpu.VMEM((2, 2, C // 2, PIECE), BF16),
            pltpu.VMEM((2, 2, C // 2, PIECE), BF16),
            pltpu.VMEM((2, 2, C // 2, PIECE), BF16),
            pltpu.VMEM((2, 2, C // 2, PIECE), BF16),
            pltpu.VMEM((2, 2, C // 2, PIECE), BF16),
            dma((9,)),
            dma((HEADS,)),
            dma((HEADS,)),
            dma((HALF,)),
            dma((NZ,)),
            dma((NX,)),
            dma((NX,)),
            dma((NZ,)),
            dma((HEADS,)),
            dma((HALF,)),
            dma((10,)),
            dma((10,)),
        ],
        compiler_params=pltpu.CompilerParams(
            collective_id=0, has_side_effects=True, vmem_limit_bytes=62 * 2**20
        ),
        cost_estimate=pl.CostEstimate(
            flops=2 * 10**9, bytes_accessed=6 * 10**6, transcendentals=10**6
        ),
    )(q, k, v, gate, decay, rate, init, gain.reshape(1, C), weight)


def solution(mesh):
    return jax.shard_map(
        on_device,
        mesh=mesh,
        in_specs=(
            P("seq", "head"),
            P("seq", "head"),
            P("seq", "head"),
            P("seq", "head"),
            P("head", "seq"),
            P("head", "seq"),
            P("head", None, None),
            P(),
            P("head", None),
        ),
        out_specs=P("seq", "head"),
        check_vma=False,
    )
```
